32 devices in a mesh: arc: 8 (over y, x, core), mas: 4 (over z).
Axes of the slice: x: 2, y: 2, z: 4, core: 2. Of those that a mesh axis runs over, the one named last changes fastest.
Arguments:
- jac: bfloat16 [8, 16, 1024, 256], P('arc', 'mas')
- resid: float32 [8, 1024], P('arc'), may hold values from -6 to 6
- counts: int32 [8], P('arc'), may hold values from 512 to 1024
- vis: int32 [8, 16], P('arc'), may hold values from 0 to 39, as said below
- xcur: float32 [40, 256], P('mas'), may hold values from -6 to 6
- damp: float32 [40, 256], P('mas'), may hold values from 2 to 20
Outputs:
- updated: float32 [40, 256], P('mas')
- postfit: float32 [8, 1024], P('arc', 'mas')
The draws below stay inside these ranges and needn't reach their ends.
Inputs may be any that keep to these rules, and one draw needn't show every extreme that they name: `vis`: each row names 16 distinct blocks; block b is held by index b // 10 of mas.
All inputs are finite; a program needn't handle non-finite values.
Results may differ from the reference program's by a relative error of at most 0.0003.
Values sent between devices are 32-bit elements; how exact they have to be, the bound alone decides.
A program may use at most 64 MiB of HBM per device.

```python
import math
import jax
import jax.numpy as jnp
from jax import lax

MB = 256
BLK_DEV = 10
VIS_PER = 4
ROWS = 1024
ITERS = 4
NBLK = 40
VIS = 16
ARCS = 8


def draw_jac(key, part):
    first, second = jax.random.split(key, 2)
    shape = (ARCS, VIS, ROWS, MB)
    base = jax.random.normal(first, shape, jnp.float32)
    col_scale = jnp.exp(jax.random.uniform(second, (ARCS, VIS, 1, MB), jnp.float32, 0.0, math.log(10.0)))
    return (0.02 * base * col_scale).astype(jnp.bfloat16)


def draw_counts(key, part):
    first, second = jax.random.split(key)
    drawn = jax.random.randint(first, (ARCS,), ROWS // 2, ROWS + 1)
    longest = jax.random.randint(second, (), 0, ARCS)
    return jnp.where(jnp.arange(ARCS) == longest, ROWS, drawn).astype(jnp.int32)


def draw_vis(key, part):
    first, second, third = jax.random.split(key, 3)
    owners = NBLK // BLK_DEV
    centre = jax.random.permutation(first, ARCS) % owners
    holder = jnp.arange(owners)
    offset = (holder[None, :] - centre[:, None]) % owners
    quota = jnp.where(offset == 0, 2 * VIS_PER, jnp.where(offset == 1, 0, VIS_PER))
    keys_local = jax.random.split(second, ARCS * owners)
    local = jax.vmap(lambda k: jax.random.permutation(k, BLK_DEV))(keys_local)
    local = local.reshape(ARCS, owners, BLK_DEV)[:, :, :2 * VIS_PER]
    ids = holder[None, :, None] * BLK_DEV + local
    usable = jnp.arange(2 * VIS_PER)[None, None, :] < quota[:, :, None]
    flat_ids = ids.reshape(ARCS, owners * 2 * VIS_PER)
    flat_use = usable.reshape(ARCS, owners * 2 * VIS_PER)
    order = jnp.argsort(jnp.where(flat_use, 0, 1), axis=1, stable=True)[:, :VIS]
    chosen = jnp.take_along_axis(flat_ids, order, axis=1)
    keys_mix = jax.random.split(third, ARCS)
    shuffle = jax.vmap(lambda k: jax.random.permutation(k, VIS))(keys_mix)
    return jnp.take_along_axis(chosen, shuffle, axis=1).astype(jnp.int32)


def steps_of(rng, shape, pieces, low, high):
    level, own = 1.0, jax.random.fold_in(rng, 6)
    for position, parts in pieces:
        heights = jnp.exp(jax.random.uniform(jax.random.fold_in(own, position), (parts,), jnp.float32, low / len(pieces), high / len(pieces)))
        level = level * jnp.repeat(heights, shape[position] // parts).reshape([-1 if axis == position else 1 for axis in range(len(shape))])
    return level


def noise(key, dims, scale, bound, shards=(), dtype=jnp.bfloat16):
    values = jax.random.normal(key, dims, jnp.float32) * scale
    if len(shards) > 0:
        values = steps_of(key, dims, shards, -0.22, 0.18) * values
    return jnp.clip(values, min=-bound, max=bound).astype(dtype)


def setup_inputs(seed: int = 0) -> dict:
    arg_keys = jax.random.split(jax.random.key(seed), 7)
    return {
        "jac": draw_jac(jax.random.fold_in(arg_keys[6], 71), 0),
        "resid": noise(arg_keys[1], (ARCS, ROWS), 1.0, 6.0, ((0, 8),), jnp.float32),
        "counts": draw_counts(jax.random.fold_in(arg_keys[6], 71), 0),
        "vis": draw_vis(jax.random.fold_in(arg_keys[6], 71), 0),
        "xcur": noise(arg_keys[4], (NBLK, MB), 1.0, 6.0, ((0, 4),), jnp.float32),
        "damp": jnp.clip(jnp.exp(math.log(20.0) - 2.3025851 * jax.random.uniform(arg_keys[5], (NBLK, MB), jnp.float32) ** steps_of(arg_keys[5], (NBLK, MB), ((0, 4),), -0.2, 0.2)), 2.0, 20.0),
    }


def reference(jac, resid, counts, vis, xcur, damp):
    valid_rows = jnp.arange(ROWS)[None, :] < counts[:, None]
    prefit = jnp.where(valid_rows, resid, 0.0)

    def forward(field):
        def one_arc(pair):
            partials, ids = pair
            picked = jnp.take(field, ids, axis=0)
            return jnp.einsum("vrm,vm->r", partials.astype(jnp.float32), picked, precision=lax.Precision.HIGHEST)
        image = lax.map(one_arc, (jac, vis))
        return jnp.where(valid_rows, image, 0.0)

    def backward(row_values):
        def one_arc(pair):
            partials, values = pair
            return jnp.einsum("vrm,r->vm", partials.astype(jnp.float32), values, precision=lax.Precision.HIGHEST)
        terms = lax.map(one_arc, (jac, row_values))
        total = jnp.zeros((NBLK, MB), jnp.float32)
        return total.at[vis.reshape(-1)].add(terms.reshape(-1, MB))

    rhs = backward(prefit)
    delta = jnp.zeros((NBLK, MB), jnp.float32)
    remain = rhs
    direction = rhs
    norm_now = jnp.sum(remain * remain)
    for iteration in range(ITERS):
        applied = backward(forward(direction)) + damp * direction
        step_len = norm_now / jnp.sum(direction * applied)
        delta = delta + step_len * direction
        remain = remain - step_len * applied
        norm_next = jnp.sum(remain * remain)
        direction = remain + (norm_next / norm_now) * direction
        norm_now = norm_next
    postfit = prefit - forward(delta)
    return xcur + delta, postfit
```

```python
import functools

import jax
import jax.numpy as jnp
from jax import lax
from jax.experimental import pallas as pl
from jax.experimental.pallas import tpu as pltpu
from jax.sharding import PartitionSpec as P

ITERS = 4
LANES = 128
F32 = jnp.float32
BF16 = jnp.bfloat16
MESH = pl.DeviceIdType.MESH


def parts_of(x):
    hi = x.astype(BF16).astype(F32)
    rest = x - hi
    mid = rest.astype(BF16).astype(F32)
    return hi, mid, rest - mid


def split_rows(x):
    hi, mid, lo = parts_of(x)
    row = lax.broadcasted_iota(jnp.int32, (16, x.shape[1]), 0)
    zero = jnp.zeros((16, x.shape[1]), F32)
    stacked = jnp.where(row == 0, hi, jnp.where(row == 1, mid, jnp.where(row == 2, lo, zero)))
    return stacked.astype(BF16)


def total_of(x):
    return jnp.sum(jnp.sum(x, axis=0, keepdims=True), axis=1, keepdims=True)


def kernel(
    arcs, mas,
    counts, vis, jac_hbm, resid, xcur, damp,
    updated, postfit,
    jac, terms, images, damps, idrows, squares, field, picker, dampfield,
    jac_sem, z_send, z_recv, p_send, p_recv, a_send, a_recv, s_send, s_recv,
):
    arc = lax.axis_index("arc")
    pos = lax.axis_index("mas")
    slots, rows = jac.shape[0], jac.shape[1]
    held = damp.shape[0]
    blocks = held * mas
    halves = 2

    z_peers = [{"mas": lax.rem(pos + k, mas)} for k in range(1, mas)]
    p_peers = [{"arc": lax.rem(arc + k, arcs)} for k in range(1, arcs)]

    barrier = pltpu.get_barrier_semaphore()
    for peer in z_peers + p_peers:
        pl.semaphore_signal(barrier, inc=1, device_id=peer, device_id_type=MESH)

    loads = [
        pltpu.make_async_copy(jac_hbm.at[0, v], jac.at[v], jac_sem.at[v]) for v in range(slots)
    ]
    for load in loads:
        load.start()

    def push(peers, ref, send_sem, recv_sem):
        for peer in peers:
            pltpu.make_async_remote_copy(
                src_ref=ref, dst_ref=ref, send_sem=send_sem, recv_sem=recv_sem,
                device_id=peer, device_id_type=MESH,
            ).start()

    def take(ref, sem):
        pltpu.make_async_copy(ref, ref, sem).wait()

    valid = lax.broadcasted_iota(jnp.int32, (1, rows), 1) < counts[0]
    prefit = jnp.where(valid, resid[...], 0.0)

    lane_count = arcs * mas * halves * slots
    lane = lax.broadcasted_iota(jnp.int32, (1, lane_count), 1)
    per_dev = halves * slots
    slot_of = lax.rem(lane // per_dev, mas) * slots + lax.rem(lane, slots)
    named = jnp.zeros((1, lane_count), F32)
    for s in range(mas * slots):
        named = jnp.where(slot_of == s, vis[0, s].astype(F32), named)
    named = jnp.where(lane // (per_dev * mas) == arc, named, 0.0)
    idrows[arc] = named
    damps[pos] = damp[...]

    def backward(step, row_values, waits):
        w = split_rows(row_values)
        for v in range(slots):
            if waits:
                loads[v].wait()
            out = jnp.dot(w, jac[v], preferred_element_type=F32)
            out = jnp.sum(out[0:8], axis=0, keepdims=True)
            for h in range(halves):
                terms[step, arc, pos, pl.ds(h * slots + v, 1), :] = out[:, h * LANES:(h + 1) * LANES]

    def spread_start(step):
        push(z_peers, terms.at[step, arc, pos], z_send.at[step], z_recv.at[step])

    def spread_finish(step):
        take(terms.at[step, 0, pl.ds(0, mas - 1)], z_recv.at[step])
        push(p_peers, terms.at[step, arc], p_send.at[step], p_recv.at[step])

    def collect(step):
        take(terms.at[step, pl.ds(0, arcs - 1)], p_recv.at[step])
        every = terms[step].reshape(lane_count, LANES)
        chosen = picker[...]
        total = None
        for part in parts_of(every):
            add = jnp.dot(chosen, part.astype(BF16), preferred_element_type=F32)
            total = add if total is None else total + add
        return total

    def forward(step, direction):
        field[...] = direction
        image = None
        for v in range(slots):
            block = vis[0, pos * slots + v]
            value = jnp.concatenate(
                [field[pl.ds(block + h * blocks, 1), :] for h in range(halves)], axis=1
            )
            add = lax.dot_general(
                split_rows(value), jac[v], (((1,), (1,)), ((), ())), preferred_element_type=F32
            )
            image = add if image is None else image + add
        images[step, pos] = jnp.sum(image[0:8], axis=0, keepdims=True)
        push(z_peers, images.at[step, pos], a_send.at[step], a_recv.at[step])
        take(images.at[step, pl.ds(0, mas - 1)], a_recv.at[step])
        return jnp.where(valid, jnp.sum(images[step], axis=0), 0.0)

    backward(0, prefit, True)
    pl.semaphore_wait(barrier, mas + arcs - 2)
    spread_start(0)
    push(p_peers, idrows.at[arc], s_send.at[0], s_recv.at[0])
    push(z_peers, damps.at[pos], s_send.at[1], s_recv.at[1])
    spread_finish(0)

    take(idrows.at[pl.ds(0, arcs - 1)], s_recv.at[0])
    names = jnp.sum(idrows[...], axis=0).astype(jnp.int32)
    names = names + lax.rem(lane // slots, halves) * blocks
    target = lax.broadcasted_iota(jnp.int32, (halves * blocks, lane_count), 0)
    picker[...] = jnp.where(target == names, 1.0, 0.0).astype(BF16)
    take(damps.at[pl.ds(0, mas - 1)], s_recv.at[1])
    for k in range(mas):
        for h in range(halves):
            dampfield[pl.ds(h * blocks + k * held, held), :] = damps[k, :, h * LANES:(h + 1) * LANES]

    remain = collect(0)
    direction = remain
    norm_now = total_of(remain * remain)
    delta = jnp.zeros_like(remain)
    change = jnp.zeros((1, rows), F32)
    for step in range(ITERS):
        image = forward(step, direction)
        damped = dampfield[...] * direction
        if step < ITERS - 1:
            backward(step + 1, image, False)
            spread_start(step + 1)
            spread_finish(step + 1)
            applied = collect(step + 1) + damped
            step_len = norm_now / total_of(direction * applied)
            delta = delta + step_len * direction
            change = change + step_len * image
            remain = remain - step_len * applied
            norm_next = total_of(remain * remain)
            direction = remain + norm_next / norm_now * direction
            norm_now = norm_next
        else:
            power = image * image
            share = power[:, 0:LANES]
            for k in range(1, rows // LANES):
                share = share + power[:, k * LANES:(k + 1) * LANES]
            squares[arc] = share
            push(p_peers, squares.at[arc], s_send.at[2], s_recv.at[2])
            own = total_of(direction * damped)
            take(squares.at[pl.ds(0, arcs - 1)], s_recv.at[2])
            step_len = norm_now / (total_of(jnp.sum(squares[...], axis=0)) + own)
            delta = delta + step_len * direction
            change = change + step_len * image

    mine = jnp.zeros((held, LANES * halves), F32)
    for k in range(mas):
        piece = jnp.concatenate(
            [delta[h * blocks + k * held:h * blocks + (k + 1) * held, :] for h in range(halves)], axis=1
        )
        mine = jnp.where(pos == k, piece, mine)
    updated[...] = xcur[...] + mine
    share_rows = rows // mas
    after = prefit - change
    kept = jnp.zeros((1, share_rows), F32)
    for k in range(mas):
        kept = jnp.where(pos == k, after[:, k * share_rows:(k + 1) * share_rows], kept)
    postfit[...] = kept

    for step in range(ITERS):
        take(terms.at[step, 0, pl.ds(0, mas - 1)], z_send.at[step])
        take(terms.at[step, pl.ds(0, arcs - 1)], p_send.at[step])
        take(images.at[step, pl.ds(0, mas - 1)], a_send.at[step])
    take(idrows.at[pl.ds(0, arcs - 1)], s_send.at[0])
    take(damps.at[pl.ds(0, mas - 1)], s_send.at[1])
    take(squares.at[pl.ds(0, arcs - 1)], s_send.at[2])


def per_device(arcs, mas, jac, resid, counts, vis, xcur, damp):
    slots, rows, width = jac.shape[1:]
    held = damp.shape[0]
    blocks = held * mas
    lane_count = arcs * mas * 2 * slots
    smem = pl.BlockSpec(memory_space=pltpu.SMEM)
    vmem = pl.BlockSpec(memory_space=pltpu.VMEM)
    dma = pltpu.SemaphoreType.DMA
    return pl.pallas_call(
        functools.partial(kernel, arcs, mas),
        out_shape=(
            jax.ShapeDtypeStruct((held, width), F32),
            jax.ShapeDtypeStruct((1, rows // mas), F32),
        ),
        in_specs=[smem, smem, pl.BlockSpec(memory_space=pl.ANY), vmem, vmem, vmem],
        out_specs=(vmem, vmem),
        scratch_shapes=[
            pltpu.VMEM((slots, rows, width), BF16),
            pltpu.VMEM((ITERS, arcs, mas, 2 * slots, LANES), F32),
            pltpu.VMEM((ITERS, mas, 1, rows), F32),
            pltpu.VMEM((mas, held, width), F32),
            pltpu.VMEM((arcs, 1, lane_count), F32),
            pltpu.VMEM((arcs, 1, LANES), F32),
            pltpu.VMEM((2 * blocks, LANES), F32),
            pltpu.VMEM((2 * blocks, lane_count), BF16),
            pltpu.VMEM((2 * blocks, LANES), F32),
            dma((slots,)),
            dma((ITERS,)), dma((ITERS,)),
            dma((ITERS,)), dma((ITERS,)),
            dma((ITERS,)), dma((ITERS,)),
            dma((3,)), dma((3,)),
        ],
        compiler_params=pltpu.CompilerParams(
            collective_id=0, has_side_effects=True, vmem_limit_bytes=48 * 1024 * 1024
        ),
    )(counts, vis, jac, resid, xcur, damp)


def solution(mesh):
    return jax.shard_map(
        functools.partial(per_device, mesh.shape["arc"], mesh.shape["mas"]),
        mesh=mesh,
        in_specs=(
            P("arc", "mas", None, None),
            P("arc", None),
            P("arc"),
            P("arc", None),
            P("mas", None),
            P("mas", None),
        ),
        out_specs=(P("mas", None), P("arc", "mas")),
        check_vma=False,
    )
```

```python
import functools

import jax
import jax.numpy as jnp
from jax import lax
from jax.experimental import pallas as pl
from jax.experimental.pallas import tpu as pltpu
from jax.sharding import PartitionSpec as P

ITERS = 4
LANES = 128
F32 = jnp.float32
BF16 = jnp.bfloat16
MESH = pl.DeviceIdType.MESH


def parts_of(x):
    hi = x.astype(BF16).astype(F32)
    rest = x - hi
    mid = rest.astype(BF16).astype(F32)
    return hi, mid, rest - mid


def split_rows(x):
    hi, mid, lo = parts_of(x)
    row = lax.broadcasted_iota(jnp.int32, (16, x.shape[1]), 0)
    zero = jnp.zeros((16, x.shape[1]), F32)
    stacked = jnp.where(row == 0, hi, jnp.where(row == 1, mid, jnp.where(row == 2, lo, zero)))
    return stacked.astype(BF16)


def total_of(x):
    return jnp.sum(jnp.sum(x, axis=0, keepdims=True), axis=1, keepdims=True)


def kernel(
    arcs, mas,
    counts, vis, jac_hbm, resid_hbm, xcur_hbm, damp_hbm,
    updated, postfit,
    jac, resid, xcur, terms, images, damps, idrows, squares, field, picker, dampfield,
    jac_sem, in_sem, p_send, p_recv, a_send, a_recv, s_send, s_recv,
):
    arc = lax.axis_index("arc")
    pos = lax.axis_index("mas")
    slots, rows = jac.shape[0], jac.shape[1]
    held = damp_hbm.shape[0]
    blocks = held * mas
    halves = 2

    z_peers = [{"mas": lax.rem(pos + k, mas)} for k in range(1, mas)]
    p_peers = [{"arc": lax.rem(arc + k, arcs)} for k in range(1, arcs)]

    devices = arcs * mas
    me = arc * mas + pos

    def each_peer(act):
        def one(k, carry):
            other = lax.rem(me + k, devices)
            act({"arc": other // mas, "mas": lax.rem(other, mas)})
            return carry
        if devices <= 32:
            for k in range(1, devices):
                one(k, 0)
        else:
            lax.fori_loop(1, devices, one, 0)

    barrier = pltpu.get_barrier_semaphore()
    each_peer(lambda peer: pl.semaphore_signal(barrier, inc=1, device_id=peer, device_id_type=MESH))

    loads = [
        pltpu.make_async_copy(jac_hbm.at[0, v], jac.at[v], jac_sem.at[v]) for v in range(slots)
    ]
    small = [
        pltpu.make_async_copy(resid_hbm, resid, in_sem.at[0]),
        pltpu.make_async_copy(xcur_hbm, xcur, in_sem.at[1]),
        pltpu.make_async_copy(damp_hbm, damps.at[pos], in_sem.at[2]),
    ]
    for load in small + loads:
        load.start()

    def push(peers, ref, send_sem, recv_sem):
        for peer in peers:
            pltpu.make_async_remote_copy(
                src_ref=ref, dst_ref=ref, send_sem=send_sem, recv_sem=recv_sem,
                device_id=peer, device_id_type=MESH,
            ).start()

    def take(ref, sem):
        pltpu.make_async_copy(ref, ref, sem).wait()

    small[0].wait()
    valid = lax.broadcasted_iota(jnp.int32, (1, rows), 1) < counts[0]
    prefit = jnp.where(valid, resid[...], 0.0)

    lane_count = arcs * mas * halves * slots
    lane = lax.broadcasted_iota(jnp.int32, (1, lane_count), 1)
    per_dev = halves * slots
    slot_of = lax.rem(lane // per_dev, mas) * slots + lax.rem(lane, slots)
    named = jnp.zeros((1, lane_count), F32)
    for s in range(mas * slots):
        named = jnp.where(slot_of == s, vis[0, s].astype(F32), named)
    named = jnp.where(lane // (per_dev * mas) == arc, named, 0.0)
    idrows[arc] = named

    def backward(step, row_values, waits):
        w = split_rows(row_values)
        for v in range(slots):
            if waits:
                loads[v].wait()
            out = jnp.dot(w, jac[v], preferred_element_type=F32)
            out = jnp.sum(out[0:8], axis=0, keepdims=True)
            for h in range(halves):
                terms[step, me, pl.ds(h * slots + v, 1), :] = out[:, h * LANES:(h + 1) * LANES]

    def spread_start(step):
        mine = terms.at[step, me]
        each_peer(lambda peer: push([peer], mine, p_send.at[step], p_recv.at[step]))

    def collect(step):
        take(terms.at[step, pl.ds(0, devices - 1)], p_recv.at[step])
        every = terms[step].reshape(lane_count, LANES)
        chosen = picker[...]
        total = None
        for part in parts_of(every):
            add = jnp.dot(chosen, part.astype(BF16), preferred_element_type=F32)
            total = add if total is None else total + add
        return total

    def forward(step, direction):
        field[...] = direction
        image = None
        for v in range(slots):
            block = vis[0, pos * slots + v]
            value = jnp.concatenate(
                [field[pl.ds(block + h * blocks, 1), :] for h in range(halves)], axis=1
            )
            add = lax.dot_general(
                split_rows(value), jac[v], (((1,), (1,)), ((), ())), preferred_element_type=F32
            )
            image = add if image is None else image + add
        images[step, pos] = jnp.sum(image[0:8], axis=0, keepdims=True)
        push(z_peers, images.at[step, pos], a_send.at[step], a_recv.at[step])
        take(images.at[step, pl.ds(0, mas - 1)], a_recv.at[step])
        return jnp.where(valid, jnp.sum(images[step], axis=0), 0.0)

    backward(0, prefit, True)
    pl.semaphore_wait(barrier, devices - 1)
    spread_start(0)
    push(p_peers, idrows.at[arc], s_send.at[0], s_recv.at[0])
    small[2].wait()
    push(z_peers, damps.at[pos], s_send.at[1], s_recv.at[1])

    take(idrows.at[pl.ds(0, arcs - 1)], s_recv.at[0])
    names = jnp.sum(idrows[...], axis=0).astype(jnp.int32)
    names = names + lax.rem(lane // slots, halves) * blocks
    target = lax.broadcasted_iota(jnp.int32, (halves * blocks, lane_count), 0)
    picker[...] = jnp.where(target == names, 1.0, 0.0).astype(BF16)
    take(damps.at[pl.ds(0, mas - 1)], s_recv.at[1])
    for k in range(mas):
        for h in range(halves):
            dampfield[pl.ds(h * blocks + k * held, held), :] = damps[k, :, h * LANES:(h + 1) * LANES]

    remain = collect(0)
    direction = remain
    norm_now = total_of(remain * remain)
    delta = jnp.zeros_like(remain)
    change = jnp.zeros((1, rows), F32)
    for step in range(ITERS):
        image = forward(step, direction)
        damped = dampfield[...] * direction
        if step < ITERS - 1:
            backward(step + 1, image, False)
            spread_start(step + 1)
            applied = collect(step + 1) + damped
            step_len = norm_now / total_of(direction * applied)
            delta = delta + step_len * direction
            change = change + step_len * image
            remain = remain - step_len * applied
            norm_next = total_of(remain * remain)
            direction = remain + norm_next / norm_now * direction
            norm_now = norm_next
        else:
            power = image * image
            share = power[:, 0:LANES]
            for k in range(1, rows // LANES):
                share = share + power[:, k * LANES:(k + 1) * LANES]
            squares[arc] = share
            push(p_peers, squares.at[arc], s_send.at[2], s_recv.at[2])
            own = total_of(direction * damped)
            take(squares.at[pl.ds(0, arcs - 1)], s_recv.at[2])
            step_len = norm_now / (total_of(jnp.sum(squares[...], axis=0)) + own)
            delta = delta + step_len * direction
            change = change + step_len * image

    mine = jnp.zeros((held, LANES * halves), F32)
    for k in range(mas):
        piece = jnp.concatenate(
            [delta[h * blocks + k * held:h * blocks + (k + 1) * held, :] for h in range(halves)], axis=1
        )
        mine = jnp.where(pos == k, piece, mine)
    small[1].wait()
    updated[...] = xcur[...] + mine
    share_rows = rows // mas
    after = prefit - change
    kept = jnp.zeros((1, share_rows), F32)
    for k in range(mas):
        kept = jnp.where(pos == k, after[:, k * share_rows:(k + 1) * share_rows], kept)
    postfit[...] = kept

    for step in range(ITERS):
        take(terms.at[step, pl.ds(0, devices - 1)], p_send.at[step])
        take(images.at[step, pl.ds(0, mas - 1)], a_send.at[step])
    take(idrows.at[pl.ds(0, arcs - 1)], s_send.at[0])
    take(damps.at[pl.ds(0, mas - 1)], s_send.at[1])
    take(squares.at[pl.ds(0, arcs - 1)], s_send.at[2])


def per_device(arcs, mas, jac, resid, counts, vis, xcur, damp):
    slots, rows, width = jac.shape[1:]
    held = damp.shape[0]
    blocks = held * mas
    lane_count = arcs * mas * 2 * slots
    smem = pl.BlockSpec(memory_space=pltpu.SMEM)
    vmem = pl.BlockSpec(memory_space=pltpu.VMEM)
    dma = pltpu.SemaphoreType.DMA
    return pl.pallas_call(
        functools.partial(kernel, arcs, mas),
        out_shape=(
            jax.ShapeDtypeStruct((held, width), F32),
            jax.ShapeDtypeStruct((1, rows // mas), F32),
        ),
        in_specs=[smem, smem] + [pl.BlockSpec(memory_space=pl.ANY)] * 4,
        out_specs=(vmem, vmem),
        scratch_shapes=[
            pltpu.VMEM((slots, rows, width), BF16),
            pltpu.VMEM((1, rows), F32),
            pltpu.VMEM((held, width), F32),
            pltpu.VMEM((ITERS, arcs * mas, 2 * slots, LANES), F32),
            pltpu.VMEM((ITERS, mas, 1, rows), F32),
            pltpu.VMEM((mas, held, width), F32),
            pltpu.VMEM((arcs, 1, lane_count), F32),
            pltpu.VMEM((arcs, 1, LANES), F32),
            pltpu.VMEM((2 * blocks, LANES), F32),
            pltpu.VMEM((2 * blocks, lane_count), BF16),
            pltpu.VMEM((2 * blocks, LANES), F32),
            dma((slots,)),
            dma((3,)),
            dma((ITERS,)), dma((ITERS,)),
            dma((ITERS,)), dma((ITERS,)),
            dma((3,)), dma((3,)),
        ],
        compiler_params=pltpu.CompilerParams(
            collective_id=0, has_side_effects=True, vmem_limit_bytes=62 * 1024 * 1024
        ),
    )(counts, vis, jac, resid, xcur, damp)


def solution(mesh):
    return jax.shard_map(
        functools.partial(per_device, mesh.shape["arc"], mesh.shape["mas"]),
        mesh=mesh,
        in_specs=(
            P("arc", "mas", None, None),
            P("arc", None),
            P("arc"),
            P("arc", None),
            P("mas", None),
            P("mas", None),
        ),
        out_specs=(P("mas", None), P("arc", "mas")),
        check_vma=False,
    )
```

```python
import functools

import jax
import jax.numpy as jnp
from jax import lax
from jax.experimental import pallas as pl
from jax.experimental.pallas import tpu as pltpu
from jax.sharding import PartitionSpec as P

ITERS = 4
LANES = 128
F32 = jnp.float32
BF16 = jnp.bfloat16
MESH = pl.DeviceIdType.MESH


def parts_of(x):
    hi = x.astype(BF16).astype(F32)
    rest = x - hi
    mid = rest.astype(BF16).astype(F32)
    return hi, mid, rest - mid


def split_rows(x):
    hi, mid, lo = parts_of(x)
    row = lax.broadcasted_iota(jnp.int32, (16, x.shape[1]), 0)
    zero = jnp.zeros((16, x.shape[1]), F32)
    stacked = jnp.where(row == 0, hi, jnp.where(row == 1, mid, jnp.where(row == 2, lo, zero)))
    return stacked.astype(BF16)


def total_of(x):
    return jnp.sum(jnp.sum(x, axis=0, keepdims=True), axis=1, keepdims=True)


def kernel(
    arcs, mas,
    counts_hbm, vis_hbm, jac_hbm, resid_hbm, xcur_hbm, damp_hbm,
    updated, postfit,
    counts, vis, jac, resid, xcur, terms, images, damps, idrows, everyone, field, picker, dampfield,
    jac_sem, in_sem, p_send, p_recv, a_send, a_recv, s_send, s_recv,
):
    arc = lax.axis_index("arc")
    pos = lax.axis_index("mas")
    slots, rows = jac.shape[0], jac.shape[1]
    held = damp_hbm.shape[0]
    blocks = held * mas
    halves = 2

    z_peers = [{"mas": lax.rem(pos + k, mas)} for k in range(1, mas)]
    p_peers = [{"arc": lax.rem(arc + k, arcs)} for k in range(1, arcs)]

    devices = arcs * mas
    me = arc * mas + pos

    def each_peer(act):
        def one(k, carry):
            other = lax.rem(me + k, devices)
            act({"arc": other // mas, "mas": lax.rem(other, mas)})
            return carry
        if devices <= 32:
            for k in range(1, devices):
                one(k, 0)
        else:
            lax.fori_loop(1, devices, one, 0)

    barrier = pltpu.get_barrier_semaphore()
    each_peer(lambda peer: pl.semaphore_signal(barrier, inc=1, device_id=peer, device_id_type=MESH))

    loads = [
        pltpu.make_async_copy(jac_hbm.at[0, v], jac.at[v], jac_sem.at[v]) for v in range(slots)
    ]
    small = [
        pltpu.make_async_copy(vis_hbm, vis, in_sem.at[3]),
        pltpu.make_async_copy(counts_hbm, counts, in_sem.at[4]),
        pltpu.make_async_copy(resid_hbm, resid, in_sem.at[0]),
        pltpu.make_async_copy(xcur_hbm, xcur, in_sem.at[1]),
        pltpu.make_async_copy(damp_hbm, damps.at[pos], in_sem.at[2]),
    ]
    for load in small + loads:
        load.start()

    def push(peers, ref, send_sem, recv_sem):
        for peer in peers:
            pltpu.make_async_remote_copy(
                src_ref=ref, dst_ref=ref, send_sem=send_sem, recv_sem=recv_sem,
                device_id=peer, device_id_type=MESH,
            ).start()

    def take(ref, sem):
        pltpu.make_async_copy(ref, ref, sem).wait()

    small[2].wait()
    small[0].wait()
    small[1].wait()
    valid = lax.broadcasted_iota(jnp.int32, (1, rows), 1) < counts[0]
    prefit = jnp.where(valid, resid[...], 0.0)

    lane_count = arcs * mas * halves * slots
    lane = lax.broadcasted_iota(jnp.int32, (1, lane_count), 1)
    per_dev = halves * slots
    slot_of = lax.rem(lane // per_dev, mas) * slots + lax.rem(lane, slots)
    named = jnp.zeros((1, lane_count), F32)
    for s in range(mas * slots):
        named = jnp.where(slot_of == s, vis[0, s].astype(F32), named)
    named = jnp.where(lane // (per_dev * mas) == arc, named, 0.0)
    idrows[arc] = named

    def backward(step, row_values, waits):
        w = split_rows(row_values)
        for v in range(slots):
            if waits:
                loads[v].wait()
            out = jnp.dot(w, jac[v], preferred_element_type=F32)
            out = jnp.sum(out[0:8], axis=0, keepdims=True)
            for h in range(halves):
                terms[step, me, pl.ds(h * slots + v, 1), :] = out[:, h * LANES:(h + 1) * LANES]

    def spread_start(step):
        mine = terms.at[step, me]
        each_peer(lambda peer: push([peer], mine, p_send.at[step], p_recv.at[step]))

    def collect(step):
        take(terms.at[step, pl.ds(0, devices - 1)], p_recv.at[step])
        every = terms[step].reshape(lane_count, LANES)
        chosen = picker[...]
        total = None
        for part in parts_of(every):
            add = jnp.dot(chosen, part.astype(BF16), preferred_element_type=F32)
            total = add if total is None else total + add
        return total

    def forward(step, direction):
        field[...] = direction
        image = None
        for v in range(slots):
            block = vis[0, pos * slots + v]
            value = jnp.concatenate(
                [field[pl.ds(block + h * blocks, 1), :] for h in range(halves)], axis=1
            )
            add = lax.dot_general(
                split_rows(value), jac[v], (((1,), (1,)), ((), ())), preferred_element_type=F32
            )
            image = add if image is None else image + add
        summed = jnp.sum(image[0:8], axis=0, keepdims=True)
        if step == ITERS - 1:
            everyone[me] = jnp.where(valid, summed, 0.0)
            mine = everyone.at[me]
            each_peer(lambda peer: push([peer], mine, s_send.at[2], s_recv.at[2]))
            return None
        images[step, pos] = summed
        push(z_peers, images.at[step, pos], a_send.at[step], a_recv.at[step])
        take(images.at[step, pl.ds(0, mas - 1)], a_recv.at[step])
        return jnp.where(valid, jnp.sum(images[step], axis=0), 0.0)

    backward(0, prefit, True)
    pl.semaphore_wait(barrier, devices - 1)
    spread_start(0)
    push(p_peers, idrows.at[arc], s_send.at[0], s_recv.at[0])
    small[4].wait()
    push(z_peers, damps.at[pos], s_send.at[1], s_recv.at[1])

    take(idrows.at[pl.ds(0, arcs - 1)], s_recv.at[0])
    names = jnp.sum(idrows[...], axis=0).astype(jnp.int32)
    names = names + lax.rem(lane // slots, halves) * blocks
    target = lax.broadcasted_iota(jnp.int32, (halves * blocks, lane_count), 0)
    picker[...] = jnp.where(target == names, 1.0, 0.0).astype(BF16)
    take(damps.at[pl.ds(0, mas - 1)], s_recv.at[1])
    for k in range(mas):
        for h in range(halves):
            dampfield[pl.ds(h * blocks + k * held, held), :] = damps[k, :, h * LANES:(h + 1) * LANES]

    remain = collect(0)
    direction = remain
    norm_now = total_of(remain * remain)
    delta = jnp.zeros_like(remain)
    change = jnp.zeros((1, rows), F32)
    for step in range(ITERS):
        image = forward(step, direction)
        damped = dampfield[...] * direction
        if step < ITERS - 1:
            backward(step + 1, image, False)
            spread_start(step + 1)
            applied = collect(step + 1) + damped
            step_len = norm_now / total_of(direction * applied)
            delta = delta + step_len * direction
            change = change + step_len * image
            remain = remain - step_len * applied
            norm_next = total_of(remain * remain)
            direction = remain + norm_next / norm_now * direction
            norm_now = norm_next
        else:
            own = total_of(direction * damped)
            take(everyone.at[pl.ds(0, devices - 1)], s_recv.at[2])
            power = jnp.zeros((1, rows), F32)
            image = jnp.zeros((1, rows), F32)
            for k in range(arcs):
                whole = jnp.sum(everyone[pl.ds(k * mas, mas)], axis=0)
                power = power + whole * whole
                image = jnp.where(arc == k, whole, image)
            step_len = norm_now / (total_of(power) + own)
            delta = delta + step_len * direction
            change = change + step_len * image

    mine = jnp.zeros((held, LANES * halves), F32)
    for k in range(mas):
        piece = jnp.concatenate(
            [delta[h * blocks + k * held:h * blocks + (k + 1) * held, :] for h in range(halves)], axis=1
        )
        mine = jnp.where(pos == k, piece, mine)
    small[3].wait()
    updated[...] = xcur[...] + mine
    share_rows = rows // mas
    after = prefit - change
    kept = jnp.zeros((1, share_rows), F32)
    for k in range(mas):
        kept = jnp.where(pos == k, after[:, k * share_rows:(k + 1) * share_rows], kept)
    postfit[...] = kept

    for step in range(ITERS):
        take(terms.at[step, pl.ds(0, devices - 1)], p_send.at[step])
        if step < ITERS - 1:
            take(images.at[step, pl.ds(0, mas - 1)], a_send.at[step])
    take(idrows.at[pl.ds(0, arcs - 1)], s_send.at[0])
    take(damps.at[pl.ds(0, mas - 1)], s_send.at[1])
    take(everyone.at[pl.ds(0, devices - 1)], s_send.at[2])


def per_device(arcs, mas, jac, resid, counts, vis, xcur, damp):
    slots, rows, width = jac.shape[1:]
    held = damp.shape[0]
    blocks = held * mas
    lane_count = arcs * mas * 2 * slots
    vmem = pl.BlockSpec(memory_space=pltpu.VMEM)
    dma = pltpu.SemaphoreType.DMA
    return pl.pallas_call(
        functools.partial(kernel, arcs, mas),
        out_shape=(
            jax.ShapeDtypeStruct((held, width), F32),
            jax.ShapeDtypeStruct((1, rows // mas), F32),
        ),
        in_specs=[pl.BlockSpec(memory_space=pl.ANY)] * 6,
        out_specs=(vmem, vmem),
        scratch_shapes=[
            pltpu.SMEM(counts.shape, jnp.int32),
            pltpu.SMEM(vis.shape, jnp.int32),
            pltpu.VMEM((slots, rows, width), BF16),
            pltpu.VMEM((1, rows), F32),
            pltpu.VMEM((held, width), F32),
            pltpu.VMEM((ITERS, arcs * mas, 2 * slots, LANES), F32),
            pltpu.VMEM((ITERS, mas, 1, rows), F32),
            pltpu.VMEM((mas, held, width), F32),
            pltpu.VMEM((arcs, 1, lane_count), F32),
            pltpu.VMEM((arcs * mas, 1, rows), F32),
            pltpu.VMEM((2 * blocks, LANES), F32),
            pltpu.VMEM((2 * blocks, lane_count), BF16),
            pltpu.VMEM((2 * blocks, LANES), F32),
            dma((slots,)),
            dma((5,)),
            dma((ITERS,)), dma((ITERS,)),
            dma((ITERS,)), dma((ITERS,)),
            dma((3,)), dma((3,)),
        ],
        compiler_params=pltpu.CompilerParams(
            collective_id=0, has_side_effects=True, vmem_limit_bytes=62 * 1024 * 1024
        ),
    )(counts, vis, jac, resid, xcur, damp)


def solution(mesh):
    return jax.shard_map(
        functools.partial(per_device, mesh.shape["arc"], mesh.shape["mas"]),
        mesh=mesh,
        in_specs=(
            P("arc", "mas", None, None),
            P("arc", None),
            P("arc"),
            P("arc", None),
            P("mas", None),
            P("mas", None),
        ),
        out_specs=(P("mas", None), P("arc", "mas")),
        check_vma=False,
    )
```
